32 devices in a mesh: dp: 4 (over y, core), fsdp: 8 (over z, x).
Axes of the slice: x: 2, y: 2, z: 4, core: 2. Of those that a mesh axis runs over, the one named last changes fastest.
Arguments:
- grad_q: bfloat16 [4, 8192, 8192], P('dp', 'fsdp'), may hold values from -40 to 40, as said below
- grad_k: bfloat16 [4, 8192, 1024], P('dp', 'fsdp'), may hold values from -40 to 40
- grad_v: bfloat16 [4, 8192, 1024], P('dp', 'fsdp'), may hold values from -40 to 40
- proj_q: bfloat16 [8192, 512], P('fsdp'), may hold values from -5 to 5, as said below
- proj_k: bfloat16 [8192, 512], P('fsdp'), may hold values from -5 to 5
- proj_v: bfloat16 [8192, 512], P('fsdp'), may hold values from -5 to 5
- weight_q: bfloat16 [8192, 8192], P('fsdp', 'dp'), may hold values from -4 to 4
- key_weight_matrix: bfloat16 [8192, 1024], P('fsdp', 'dp'), may hold values from -4 to 4
- value_weight_matrix: bfloat16 [8192, 1024], P('fsdp', 'dp'), may hold values from -4 to 4
- comp_q: bfloat16 [8192, 8192], P('fsdp', 'dp'), may hold values from -0.0039978027 to 0.0039978027
- key_compensation: bfloat16 [8192, 1024], P('fsdp', 'dp'), may hold values from -0.0039978027 to 0.0039978027
- value_compensation: bfloat16 [8192, 1024], P('fsdp', 'dp'), may hold values from -0.0039978027 to 0.0039978027
- avg_q: float32 [512, 8192], P('fsdp', 'dp'), may hold values from -1.5 to 1.5
- key_first_moment: float32 [512, 1024], P('fsdp', 'dp'), may hold values from -1.5 to 1.5
- value_first_moment: float32 [512, 1024], P('fsdp', 'dp'), may hold values from -1.5 to 1.5
- sq_q: float32 [512, 8192], P('fsdp', 'dp'), may hold values from 0.001 to 0.1
- key_second_moment: float32 [512, 1024], P('fsdp', 'dp'), may hold values from 0.001 to 0.1
- value_second_moment: float32 [512, 1024], P('fsdp', 'dp'), may hold values from 0.001 to 0.1
Outputs:
- new_weight_q: float32 [8192, 8192], P('fsdp', 'dp')
- new_weight_k: float32 [8192, 1024], P('fsdp', 'dp')
- new_weight_v: float32 [8192, 1024], P('fsdp', 'dp')
- new_avg_q: float32 [512, 8192], P('fsdp', 'dp')
- new_avg_k: float32 [512, 1024], P('fsdp', 'dp')
- new_avg_v: float32 [512, 1024], P('fsdp', 'dp')
- new_sq_q: float32 [512, 8192], P('fsdp', 'dp')
- new_sq_k: float32 [512, 1024], P('fsdp', 'dp')
- new_sq_v: float32 [512, 1024], P('fsdp', 'dp')
The draws below stay inside these ranges and needn't reach their ends.
Inputs may be any that keep to these rules, and one draw needn't show every extreme that they name: `grad_q`: each partial of the gradients is real-valued and of full rank. `proj_q`: projectors are real-valued and of full rank 512.
All inputs are finite; a program needn't handle non-finite values.
Results may differ from the reference program's by a relative error of at most 0.00044.
Values may be sent and summed in bfloat16 or wider, within the bound.
A program may use at most 128 MiB of HBM per device.

```python
import math
import jax
import jax.numpy as jnp
from jax import lax

MODEL_WIDTH = 8192
QUERY_OUTPUTS = 8192
KEY_VALUE_OUTS = 1024
PROJECT_RANK = 512
STEP = 10
N_DP = 4
N_FSDP = 8


def column_scales(columns):
    steps_along = jnp.arange(columns, dtype=jnp.float32) / max(columns - 1, 1)
    return jnp.exp(math.log(10.0) * steps_along)


def row_profile(key, matrix_tag):
    return jax.random.uniform(jax.random.fold_in(key, 100 + matrix_tag), (MODEL_WIDTH,), jnp.float32, 0.5, 1.0)


def gradient_sampler(key, matrix_tag, columns):
    own_key = jax.random.fold_in(key, matrix_tag)
    scales = column_scales(columns)
    row_weights = row_profile(key, matrix_tag)
    column_mix = jax.random.uniform(jax.random.fold_in(own_key, 14), (columns,), jnp.float32, -1.5, 1.5)
    coherent = 0.1 * row_weights[:, None] * column_mix[None, :]
    level_grid = jnp.exp(jax.random.uniform(jax.random.fold_in(own_key, 15), (N_FSDP, N_DP), jnp.float32, -1.5, 0.0))
    levels = jnp.repeat(jnp.repeat(level_grid, MODEL_WIDTH // N_FSDP, axis=0), columns // N_DP, axis=1)
    random_part = jax.random.truncated_normal(jax.random.fold_in(own_key, 13), -3.5, 3.5, (N_DP, MODEL_WIDTH, columns), jnp.float32)
    values = (random_part + coherent[None]) * levels[None] * scales
    return values.astype(jnp.bfloat16)


def projector_draw(key, matrix_tag):
    own_key = jax.random.fold_in(key, 10 + matrix_tag)
    scales = column_scales(PROJECT_RANK) / math.sqrt(MODEL_WIDTH)
    row_weights = row_profile(key, matrix_tag)
    rank_mix = jax.random.uniform(jax.random.fold_in(own_key, 23), (PROJECT_RANK,), jnp.float32, -1.7, 1.7)
    coherent = 0.1 * row_weights[:, None] * rank_mix[None, :]
    random_part = jax.random.truncated_normal(jax.random.fold_in(own_key, 22), -3.8, 3.8, (MODEL_WIDTH, PROJECT_RANK), jnp.float32)
    values = (random_part + coherent) * scales
    return values.astype(jnp.bfloat16)


def draw_grad_q(key, part):
    return gradient_sampler(key, 1, QUERY_OUTPUTS)


def draw_grad_k(key, part):
    return gradient_sampler(key, 2, KEY_VALUE_OUTS)


def draw_grad_v(key, part):
    return gradient_sampler(key, 3, KEY_VALUE_OUTS)


def draw_proj_q(key, part):
    return projector_draw(key, 1)


def draw_proj_k(key, part):
    return projector_draw(key, 2)


def draw_proj_v(key, part):
    return projector_draw(key, 3)


def block_levels(stream_key, shape, shards, least, high):
    factor_of, own = 1.0, jax.random.fold_in(stream_key, 6)
    for axis_at, parts in shards:
        draws = jnp.exp(jax.random.uniform(jax.random.fold_in(own, axis_at), (parts,), jnp.float32, least / len(shards), high / len(shards)))
        factor_of = factor_of * jnp.repeat(draws, shape[axis_at] // parts).reshape([-1 if axis == axis_at else 1 for axis in range(len(shape))])
    return factor_of


def normal_values(rng, extent, scale, bound, cuts=(), kind=jnp.bfloat16):
    factor_of = block_levels(rng, extent, cuts, -0.22, 0.18) if cuts else 1.0
    entries = jax.random.normal(rng, extent, jnp.float32) * scale * factor_of
    return jnp.minimum(jnp.maximum(entries, -bound), bound).astype(kind)


def setup_inputs(seed: int = 0) -> dict:
    key_list = jax.random.split(jax.random.key(seed), 19)
    return {
        "grad_q": draw_grad_q(jax.random.fold_in(key_list[18], 71), 0),
        "grad_k": draw_grad_k(jax.random.fold_in(key_list[18], 71), 0),
        "grad_v": draw_grad_v(jax.random.fold_in(key_list[18], 71), 0),
        "proj_q": draw_proj_q(jax.random.fold_in(key_list[18], 71), 0),
        "proj_k": draw_proj_k(jax.random.fold_in(key_list[18], 71), 0),
        "proj_v": draw_proj_v(jax.random.fold_in(key_list[18], 71), 0),
        "weight_q": normal_values(key_list[6], (MODEL_WIDTH, QUERY_OUTPUTS), 0.25, 4.0, ((0, 8), (1, 4))),
        "key_weight_matrix": normal_values(key_list[7], (MODEL_WIDTH, KEY_VALUE_OUTS), 0.25, 4.0, ((0, 8), (1, 4))),
        "value_weight_matrix": normal_values(key_list[8], (MODEL_WIDTH, KEY_VALUE_OUTS), 0.25, 4.0, ((0, 8), (1, 4))),
        "comp_q": jnp.clip(jax.random.uniform(key_list[9], (MODEL_WIDTH, QUERY_OUTPUTS), jnp.float32, -0.0039978027, 0.0039978027) * block_levels(key_list[9], (MODEL_WIDTH, QUERY_OUTPUTS), ((0, 8), (1, 4)), -0.4, 0.0), -0.0039978027, 0.0039978027).astype(jnp.bfloat16),
        "key_compensation": jnp.clip(jax.random.uniform(key_list[10], (MODEL_WIDTH, KEY_VALUE_OUTS), jnp.float32, -0.0039978027, 0.0039978027) * block_levels(key_list[10], (MODEL_WIDTH, KEY_VALUE_OUTS), ((0, 8), (1, 4)), -0.4, 0.0), -0.0039978027, 0.0039978027).astype(jnp.bfloat16),
        "value_compensation": jnp.clip(jax.random.uniform(key_list[11], (MODEL_WIDTH, KEY_VALUE_OUTS), jnp.float32, -0.0039978027, 0.0039978027) * block_levels(key_list[11], (MODEL_WIDTH, KEY_VALUE_OUTS), ((0, 8), (1, 4)), -0.4, 0.0), -0.0039978027, 0.0039978027).astype(jnp.bfloat16),
        "avg_q": normal_values(key_list[12], (PROJECT_RANK, QUERY_OUTPUTS), 0.1, 1.5, ((0, 8), (1, 4)), jnp.float32),
        "key_first_moment": normal_values(key_list[13], (PROJECT_RANK, KEY_VALUE_OUTS), 0.1, 1.5, ((0, 8), (1, 4)), jnp.float32),
        "value_first_moment": normal_values(key_list[14], (PROJECT_RANK, KEY_VALUE_OUTS), 0.1, 1.5, ((0, 8), (1, 4)), jnp.float32),
        "sq_q": jnp.clip(jnp.exp(math.log(0.1) - 4.6051702 * jax.random.uniform(key_list[15], (PROJECT_RANK, QUERY_OUTPUTS), jnp.float32) ** block_levels(key_list[15], (PROJECT_RANK, QUERY_OUTPUTS), ((0, 8), (1, 4)), -0.2, 0.2)), 0.001, 0.1),
        "key_second_moment": jnp.clip(jnp.exp(math.log(0.1) - 4.6051702 * jax.random.uniform(key_list[16], (PROJECT_RANK, KEY_VALUE_OUTS), jnp.float32) ** block_levels(key_list[16], (PROJECT_RANK, KEY_VALUE_OUTS), ((0, 8), (1, 4)), -0.2, 0.2)), 0.001, 0.1),
        "value_second_moment": jnp.clip(jnp.exp(math.log(0.1) - 4.6051702 * jax.random.uniform(key_list[17], (PROJECT_RANK, KEY_VALUE_OUTS), jnp.float32) ** block_levels(key_list[17], (PROJECT_RANK, KEY_VALUE_OUTS), ((0, 8), (1, 4)), -0.2, 0.2)), 0.001, 0.1),
    }


def project_sum(gradient, projector):

    def accumulate(carry, slab):
        product = lax.dot_general(projector, slab, (((0,), (0,)), ((), ())), preferred_element_type=jnp.float32)
        return (carry + product, None)
    start_sum = jnp.zeros((projector.shape[1], gradient.shape[2]), jnp.float32)
    return lax.scan(accumulate, start_sum, gradient)[0]

def adam_apply(projected, clip_factor, first_moment, second_moment):
    scaled = clip_factor * projected
    new_avg = 0.9 * first_moment + 0.1 * scaled
    new_sq = 0.95 * second_moment + 0.05 * scaled * scaled
    correct_one = 1.0 - 0.9 ** STEP
    correct_two = 1.0 - 0.95 ** STEP
    update = new_avg / correct_one / (jnp.sqrt(new_sq / correct_two) + 1e-08)
    return (new_avg, new_sq, update.astype(jnp.bfloat16))

def kahan_apply(weight, compensation, projector, update):
    delta = -0.04 * jnp.dot(projector, update, preferred_element_type=jnp.float32)
    return weight.astype(jnp.float32) + (delta + compensation.astype(jnp.float32))

def reference(grad_q, grad_k, grad_v, proj_q, proj_k, proj_v, weight_q, key_weight_matrix, value_weight_matrix, comp_q, key_compensation, value_compensation, avg_q, key_first_moment, value_first_moment, sq_q, key_second_moment, value_second_moment):
    gradients = (grad_q, grad_k, grad_v)
    projectors = (proj_q, proj_k, proj_v)
    weights = (weight_q, key_weight_matrix, value_weight_matrix)
    comps = (comp_q, key_compensation, value_compensation)
    avgs = (avg_q, key_first_moment, value_first_moment)
    squares = (sq_q, key_second_moment, value_second_moment)
    projected = [project_sum(gradient, projector) for gradient, projector in zip(gradients, projectors)]
    square_sum = jnp.zeros((), jnp.float32)
    for member in projected:
        square_sum = square_sum + jnp.sum(member * member)
    clipping_threshold = math.sqrt(PROJECT_RANK * (QUERY_OUTPUTS + 2 * KEY_VALUE_OUTS))
    clip_factor = jnp.minimum(1.0, clipping_threshold / jnp.sqrt(square_sum + 1e-06))
    new_weights, new_avgs, new_sqs = ([], [], [])
    for index_mat in range(3):
        new_avg, new_sq, update = adam_apply(projected[index_mat], clip_factor, avgs[index_mat], squares[index_mat])
        new_weights.append(kahan_apply(weights[index_mat], comps[index_mat], projectors[index_mat], update))
        new_avgs.append(new_avg)
        new_sqs.append(new_sq)
    return (new_weights[0], new_weights[1], new_weights[2], new_avgs[0], new_avgs[1], new_avgs[2], new_sqs[0], new_sqs[1], new_sqs[2])
```

```python
import functools
import math

import jax
import jax.numpy as jnp
from jax import lax
from jax.experimental import pallas as pl
from jax.experimental.pallas import tpu as pltpu
from jax.sharding import PartitionSpec as P

QUERY_OUTPUTS = 8192
KEY_VALUE_OUTS = 1024
PROJECT_RANK = 512
STEP = 10
MESH = pl.DeviceIdType.MESH
CODED = ()
SPAN = 250.0
HALF_SPAN = 125.0
PREFETCH = 3


def log2_of(n):
    return n.bit_length() - 1


def bit_reverse(i, bits):
    out = 0
    for k in range(bits):
        out = out * 2 + (i // (1 << k)) % 2
    return out


def encode(x, inverse):
    level = jnp.abs(x) * inverse
    whole = jnp.floor(level)
    code = jnp.exp2(whole - HALF_SPAN) * (1.0 + (level - whole))
    return jnp.where(x < 0.0, -code, code).astype(jnp.bfloat16)


def decode(code, step):
    y = code.astype(jnp.float32)
    size = jnp.abs(y)
    whole = jnp.floor(jnp.log2(size))
    level = (whole + (HALF_SPAN - 1.0)) + size * jnp.exp2(-whole)
    return jnp.where(y < 0.0, -level, level) * step


class Plan:
    def __init__(self, n_dp, n_fsdp, rank, depth, q_cols, kv_cols):
        self.n_dp, self.n_fsdp = n_dp, n_fsdp
        self.rank, self.depth = rank, depth
        self.q_cols, self.kv_cols = q_cols, kv_cols
        self.width = 2 * kv_cols
        self.n_q = q_cols // self.width
        self.chunks = self.n_q + 1
        self.dp_bits, self.fsdp_bits = log2_of(n_dp), log2_of(n_fsdp)
        self.rows = rank // n_fsdp
        self.half = n_dp // 2
        self.stages = self.dp_bits + self.fsdp_bits

    def order(self, c):
        dp = [("dp", k) for k in range(self.dp_bits)]
        fsdp = [("fsdp", k) for k in range(self.fsdp_bits)]
        if c % 2 == 0:
            return dp + fsdp
        return dp[:1] + fsdp + dp[1:]

    def shapes(self, c):
        out, blocks, rows = [], self.n_dp, self.rank
        for axis, _ in self.order(c):
            if axis == "dp":
                blocks //= 2
            else:
                rows //= 2
            out.append((blocks, rows))
        return out


def reduce_kernel(plan, *refs):
    (gq, gk, gv, ptq, ptk, ptv, avg_q, avg_k, avg_v, sq_q, sq_k, sq_v,
     upd_q, upd_k, upd_v, navg_q, navg_k, navg_v, nsq_q, nsq_k, nsq_v) = refs[:21]
    rest = list(refs[21:])
    (acc, grads, held, sums_dp, sums_fsdp, g_sem, s_sem, r_sem, a_send, a_recv,
     d_send, d_recv, f_send, f_recv, out_sem) = rest[:15]
    rest = rest[15:]
    landing, staging = {}, {}
    for c in range(plan.chunks):
        for s in range(plan.stages):
            landing[c, s] = rest.pop(0)
            if s in CODED:
                staging[c, s] = rest.pop(0)

    n_dp, n_fsdp, width, half = plan.n_dp, plan.n_fsdp, plan.width, plan.half
    me_d, me_f = lax.axis_index("dp"), lax.axis_index("fsdp")

    def bit_of(axis, k):
        return ((me_d if axis == "dp" else me_f) // (1 << k)) % 2

    def partner(axis, k):
        step = (1 - 2 * bit_of(axis, k)) * (1 << k)
        return (me_d + step, me_f) if axis == "dp" else (me_d, me_f + step)

    steps = [(c, j) for c in range(plan.chunks) for j in range(n_dp)]
    core = bit_of("dp", 0)

    def fetches(t):
        c, j = steps[t]
        slot = t % PREFETCH
        low = (1 - core) if j < half else core
        block = low + 2 * bit_reverse(j % half, plan.dp_bits - 1)
        if c < plan.n_q:
            start = pl.multiple_of(block * plan.q_cols + c * width, 128)
            return [pltpu.make_async_copy(
                gq.at[0, :, pl.ds(start, width)], grads.at[slot], g_sem.at[slot, 0])]
        start = pl.multiple_of(block * plan.kv_cols, 128)
        return [
            pltpu.make_async_copy(
                g.at[0, :, pl.ds(start, plan.kv_cols)],
                grads.at[slot, :, pl.ds(at * plan.kv_cols, plan.kv_cols)],
                g_sem.at[slot, at])
            for at, g in enumerate((gk, gv))
        ]

    for t in range(PREFETCH - 1):
        for copy in fetches(t):
            copy.start()

    barrier = pltpu.get_barrier_semaphore()
    for k in range(1, n_dp):
        pl.semaphore_signal(
            barrier, inc=1, device_id=((me_d + k) % n_dp, me_f), device_id_type=MESH)
    for k in range(1, n_fsdp):
        pl.semaphore_signal(
            barrier, inc=1, device_id=(me_d, (me_f + k) % n_fsdp), device_id_type=MESH)
    pl.semaphore_wait(barrier, n_dp + n_fsdp - 2)

    state = {c: (0, n_dp, 0, plan.rank) for c in range(plan.chunks)}
    copies = {}

    def start(c, s):
        axis, k = plan.order(c)[s]
        base_b, blocks, base_r, rows = state[c]
        bit = bit_of(axis, k)
        send_b, send_r = base_b, base_r
        if s == 0:
            blocks //= 2
            send_b, base_b = 0, half
        elif axis == "dp":
            blocks //= 2
            send_b, base_b = base_b + (1 - bit) * blocks, base_b + bit * blocks
        else:
            rows //= 2
            send_r, base_r = base_r + (1 - bit) * rows, base_r + bit * rows
            send_r = pl.multiple_of(send_r, 16)
            base_r = pl.multiple_of(base_r, 16)
        state[c] = (base_b, blocks, base_r, rows)
        if s in CODED:
            src = staging[c, s]
            tile = min(rows, 32)
            for b in range(blocks):
                def largest(i, top, b=b):
                    x = acc[c, send_b + b, pl.ds(pl.multiple_of(send_r + i * tile, 16), tile), :]
                    return jnp.maximum(
                        top, jnp.max(jnp.abs(x).reshape(tile // 8, 8, width), axis=0))
                top = lax.fori_loop(
                    0, rows // tile, largest, jnp.zeros((8, width), jnp.float32))
                top = jnp.max(top, axis=0, keepdims=True)
                top = (jnp.maximum(top, 1e-30) * 1.01).astype(jnp.bfloat16)
                src[b, pl.ds(rows, 16), :] = jnp.broadcast_to(top, (16, width))
                inverse = SPAN / top.astype(jnp.float32)

                def write(i, _, b=b, inverse=inverse):
                    x = acc[c, send_b + b, pl.ds(pl.multiple_of(send_r + i * tile, 16), tile), :]
                    src[b, pl.ds(pl.multiple_of(i * tile, 16), tile), :] = encode(x, inverse)
                    return 0
                lax.fori_loop(0, rows // tile, write, 0)
        else:
            src = acc.at[c, pl.ds(send_b, blocks), pl.ds(send_r, rows), :]
        copy = pltpu.make_async_remote_copy(
            src_ref=src, dst_ref=landing[c, s], send_sem=s_sem.at[c, s],
            recv_sem=r_sem.at[c, s], device_id=partner(axis, k), device_id_type=MESH)
        copy.start()
        copies[c, s] = copy

    def finish(c, s):
        base_b, blocks, base_r, rows = state[c]
        copies[c, s].wait_recv()
        got = landing[c, s]
        tile = min(rows, 32)
        for b in range(blocks):
            if s in CODED:
                step = got[b, pl.ds(rows, 16), :].astype(jnp.float32)[:1] * (1.0 / SPAN)

            def add(i, _, b=b):
                at = pl.ds(pl.multiple_of(base_r + i * tile, 16), tile)
                x = got[b, pl.ds(pl.multiple_of(i * tile, 16), tile), :]
                if s in CODED:
                    x = decode(x, step)
                acc[c, base_b + b, at, :] = acc[c, base_b + b, at, :] + x
                return 0
            lax.fori_loop(0, rows // tile, add, 0)
        if s + 1 < plan.stages:
            start(c, s + 1)

    def multiply(t):
        c, j = steps[t]
        slot = t % PREFETCH
        if t + PREFETCH - 1 < len(steps):
            for copy in fetches(t + PREFETCH - 1):
                copy.start()
        for copy in fetches(t):
            copy.wait()
        if c < plan.n_q:
            tile = min(width, 256)

            def part(i, _):
                at = pl.ds(pl.multiple_of(i * tile, 128), tile)
                acc[c, j, :, at] = jnp.dot(
                    ptq[...], grads[slot, :, at], preferred_element_type=jnp.float32)
                return 0
            lax.fori_loop(0, width // tile, part, 0)
        else:
            for at, pt in enumerate((ptk, ptv)):
                cut = pl.ds(at * plan.kv_cols, plan.kv_cols)
                acc[c, j, :, cut] = jnp.dot(
                    pt[...], grads[slot, :, cut], preferred_element_type=jnp.float32)

    for c in range(plan.chunks):
        for j in range(n_dp):
            multiply(c * n_dp + j)
            if j == half - 1:
                start(c, 0)
        if c > 0:
            finish(c - 1, 0)
    finish(plan.chunks - 1, 0)

    rest_order = [(c, s) for c in range(plan.chunks) for s in range(1, plan.stages)]
    for c, s in sorted(rest_order, key=lambda e: (1.5 * (e[0] // 2) + e[1], e[0])):
        finish(c, s)

    local = jnp.zeros((8, 128), jnp.float32)
    for c in range(plan.chunks):
        base_b, _, base_r, rows = state[c]
        x = acc[c, base_b, pl.ds(base_r, rows), :]
        folded = jnp.sum((x * x).reshape(rows // 8, 8, width), axis=0)
        for i in range(width // 128):
            local = local + folded[:, i * 128:(i + 1) * 128]

    def exchange(value, sums, n, send, recv, peer):
        sums[0] = value
        sent = []
        for k in range(1, n):
            copy = pltpu.make_async_remote_copy(
                src_ref=sums.at[0], dst_ref=sums.at[k], send_sem=send.at[k],
                recv_sem=recv.at[k], device_id=peer(k), device_id_type=MESH)
            copy.start()
            sent.append(copy)
        total = value
        for k, copy in enumerate(sent):
            copy.wait_recv()
            total = total + sums[k + 1]
        return total, sent

    total, sent_d = exchange(
        local, sums_dp, n_dp, d_send, d_recv, lambda k: ((me_d + k) % n_dp, me_f))
    total, sent_f = exchange(
        total, sums_fsdp, n_fsdp, f_send, f_recv, lambda k: (me_d, (me_f + k) % n_fsdp))
    square_sum = jnp.sum(jnp.sum(total, axis=0, keepdims=True), axis=1, keepdims=True)
    threshold = math.sqrt(PROJECT_RANK * (QUERY_OUTPUTS + 2 * KEY_VALUE_OUTS))
    clip = jnp.minimum(1.0, threshold / jnp.sqrt(square_sum + 1e-06))

    rows = plan.rows
    correct_one = 1.0 - 0.9**STEP
    correct_two = 1.0 - 0.95**STEP
    place = pl.multiple_of(bit_reverse(me_f, plan.fsdp_bits) * rows, 16)
    gathers = {}

    def gather_start(c, s):
        k = plan.fsdp_bits - 1 - s
        size = rows << s
        base = pl.multiple_of(bit_reverse(me_f, plan.fsdp_bits) // (1 << s) * size, 16)
        view = held.at[c, pl.ds(base, size), :]
        copy = pltpu.make_async_remote_copy(
            src_ref=view, dst_ref=view, send_sem=a_send.at[c, s], recv_sem=a_recv.at[c, s],
            device_id=partner("fsdp", k), device_id_type=MESH)
        copy.start()
        gathers[c, s] = copy

    def adam(c, cols, avg, sq, navg, nsq, at):
        base_b, _, base_r, _ = state[c]
        scaled = clip * acc[c, base_b, pl.ds(base_r, rows), cols]
        new_avg = 0.9 * avg[:, at] + 0.1 * scaled
        new_sq = 0.95 * sq[:, at] + 0.05 * scaled * scaled
        navg[:, at] = new_avg
        nsq[:, at] = new_sq
        update = new_avg / correct_one / (jnp.sqrt(new_sq / correct_two) + 1e-08)
        held[c, pl.ds(place, rows), cols] = update.astype(jnp.bfloat16)

    kv = plan.kv_cols
    for c in range(plan.chunks):
        if c < plan.n_q:
            adam(c, slice(0, width), avg_q, sq_q, navg_q, nsq_q, slice(c * width, (c + 1) * width))
        else:
            adam(c, slice(0, kv), avg_k, sq_k, navg_k, nsq_k, slice(0, kv))
            adam(c, slice(kv, 2 * kv), avg_v, sq_v, navg_v, nsq_v, slice(0, kv))
        gather_start(c, 0)

    stores = []

    def store(c):
        for f in range(n_fsdp):
            there = pl.ds(bit_reverse(f, plan.fsdp_bits) * rows, rows)
            here = pl.ds(f * rows, rows)
            if c < plan.n_q:
                parts = [(held.at[c, there, :], upd_q.at[here, pl.ds(c * width, width)])]
            else:
                parts = [(held.at[c, there, pl.ds(0, kv)], upd_k.at[here, :]),
                         (held.at[c, there, pl.ds(kv, kv)], upd_v.at[here, :])]
            for src, dst in parts:
                copy = pltpu.make_async_copy(src, dst, out_sem.at[len(stores)])
                copy.start()
                stores.append(copy)

    gather_order = [(c, s) for c in range(plan.chunks) for s in range(plan.fsdp_bits)]
    for c, s in sorted(gather_order, key=lambda e: (e[0] + e[1], e[0])):
        gathers[c, s].wait_recv()
        if s + 1 < plan.fsdp_bits:
            gather_start(c, s + 1)
        else:
            store(c)

    for copy in list(copies.values()) + list(gathers.values()) + sent_d + sent_f:
        copy.wait_send()
    for copy in stores:
        copy.wait()


def apply_kernel(*refs):
    proj, upd, weight, comp, out = (refs[3 * i:3 * i + 3] for i in range(5))
    for p, u, w, c, o in zip(proj, upd, weight, comp, out):
        delta = -0.04 * jnp.dot(p[...], u[...], preferred_element_type=jnp.float32)
        o[...] = w[...].astype(jnp.float32) + (delta + c[...].astype(jnp.float32))


def apply_updates(projectors, updates, weights, comps):
    rows = weights[0].shape[0]
    tile = min(rows, 128)

    def tiled(array):
        return pl.BlockSpec((tile, array.shape[1]), lambda i: (i, 0))

    def whole(array):
        return pl.BlockSpec(array.shape, lambda i: (0, 0))

    args = (*projectors, *updates, *weights, *comps)
    specs = [whole(a) if 3 <= i < 6 else tiled(a) for i, a in enumerate(args)]
    return pl.pallas_call(
        apply_kernel,
        grid=(rows // tile,),
        in_specs=specs,
        out_specs=[tiled(w) for w in weights],
        out_shape=[jax.ShapeDtypeStruct(w.shape, jnp.float32) for w in weights],
        compiler_params=pltpu.CompilerParams(vmem_limit_bytes=40 << 20),
        name="apply_updates",
    )(*args)


def shards(n_dp, n_fsdp, *args):
    gradients, projectors, weights, comps, avgs, squares = (args[3 * i:3 * i + 3] for i in range(6))
    depth, rank = projectors[0].shape
    plan = Plan(n_dp, n_fsdp, rank, depth, weights[0].shape[1], weights[1].shape[1])
    bits = plan.fsdp_bits

    def turned(projector):
        cut = projector.reshape((depth,) + (2,) * bits + (plan.rows,))
        axes = tuple(range(bits, 0, -1)) + (bits + 1, 0)
        return jnp.transpose(cut, axes).reshape(rank, depth)

    scratch = [
        pltpu.VMEM((plan.chunks, n_dp, rank, plan.width), jnp.float32),
        pltpu.VMEM((PREFETCH, depth, plan.width), jnp.bfloat16),
        pltpu.VMEM((plan.chunks, rank, plan.width), jnp.bfloat16),
        pltpu.VMEM((n_dp, 8, 128), jnp.float32),
        pltpu.VMEM((n_fsdp, 8, 128), jnp.float32),
        pltpu.SemaphoreType.DMA((PREFETCH, 2)),
        pltpu.SemaphoreType.DMA((plan.chunks, plan.stages)),
        pltpu.SemaphoreType.DMA((plan.chunks, plan.stages)),
        pltpu.SemaphoreType.DMA((plan.chunks, bits)),
        pltpu.SemaphoreType.DMA((plan.chunks, bits)),
        pltpu.SemaphoreType.DMA((n_dp,)),
        pltpu.SemaphoreType.DMA((n_dp,)),
        pltpu.SemaphoreType.DMA((n_fsdp,)),
        pltpu.SemaphoreType.DMA((n_fsdp,)),
        pltpu.SemaphoreType.DMA(((plan.n_q + 2) * n_fsdp,)),
    ]
    for c in range(plan.chunks):
        for s, (blocks, rows) in enumerate(plan.shapes(c)):
            if s in CODED:
                scratch += [pltpu.VMEM((blocks, rows + 16, plan.width), jnp.bfloat16)] * 2
            else:
                scratch.append(pltpu.VMEM((blocks, rows, plan.width), jnp.float32))

    any_spec = pl.BlockSpec(memory_space=pl.ANY)
    vmem_spec = pl.BlockSpec(memory_space=pltpu.VMEM)
    columns = [w.shape[1] for w in weights]
    moments = [jax.ShapeDtypeStruct(a.shape, jnp.float32) for a in (*avgs, *squares)]
    out = pl.pallas_call(
        functools.partial(reduce_kernel, plan),
        in_specs=[any_spec] * 3 + [vmem_spec] * 9,
        out_specs=[any_spec] * 3 + [vmem_spec] * 6,
        out_shape=[jax.ShapeDtypeStruct((rank, c), jnp.bfloat16) for c in columns] + moments,
        scratch_shapes=scratch,
        compiler_params=pltpu.CompilerParams(
            collective_id=0, has_side_effects=True, vmem_limit_bytes=62 << 20),
        name="project_reduce_gather",
    )(*gradients, *(turned(p) for p in projectors), *avgs, *squares)
    updates, new_avgs, new_sqs = out[:3], out[3:6], out[6:9]
    new_weights = apply_updates(projectors, updates, weights, comps)
    return (*new_weights, *new_avgs, *new_sqs)


def solution(mesh):
    n_dp, n_fsdp = mesh.shape["dp"], mesh.shape["fsdp"]
    grad, proj, cell = P("dp", "fsdp", None), P("fsdp", None), P("fsdp", "dp")
    in_specs = (grad,) * 3 + (proj,) * 3 + (cell,) * 12
    return jax.shard_map(
        functools.partial(shards, n_dp, n_fsdp),
        mesh=mesh, in_specs=in_specs, out_specs=(cell,) * 9, check_vma=False)
```

```python
import functools
import math

import jax
import jax.numpy as jnp
from jax import lax
from jax.experimental import pallas as pl
from jax.experimental.pallas import tpu as pltpu
from jax.sharding import PartitionSpec as P

QUERY_OUTPUTS = 8192
KEY_VALUE_OUTS = 1024
PROJECT_RANK = 512
STEP = 10
MESH = pl.DeviceIdType.MESH
CODED = (1, 2, 3, 4)
SPAN = 250.0
HALF_SPAN = 125.0
PREFETCH = 3


def log2_of(n):
    return n.bit_length() - 1


def bit_reverse(i, bits):
    out = 0
    for k in range(bits):
        out = out * 2 + (i // (1 << k)) % 2
    return out


def encode(x, inverse):
    level = jnp.abs(x) * inverse
    whole = jnp.floor(level)
    code = jnp.exp2(whole - HALF_SPAN) * (1.0 + (level - whole))
    return jnp.where(x < 0.0, -code, code).astype(jnp.bfloat16)


def decode(code, step):
    y = code.astype(jnp.float32)
    size = jnp.abs(y)
    whole = jnp.floor(jnp.log2(size))
    level = (whole + (HALF_SPAN - 1.0)) + size * jnp.exp2(-whole)
    return jnp.where(y < 0.0, -level, level) * step


def new_moments(scaled, avg, sq):
    return 0.9 * avg + 0.1 * scaled, 0.95 * sq + 0.05 * scaled * scaled


class Plan:
    def __init__(self, n_dp, n_fsdp, rank, depth, q_cols, kv_cols):
        self.n_dp, self.n_fsdp = n_dp, n_fsdp
        self.rank, self.depth = rank, depth
        self.q_cols, self.kv_cols = q_cols, kv_cols
        self.width = 2 * kv_cols
        self.n_q = q_cols // self.width
        self.chunks = self.n_q + 1
        self.dp_bits, self.fsdp_bits = log2_of(n_dp), log2_of(n_fsdp)
        self.rows = rank // n_fsdp
        self.half = n_dp // 2
        self.stages = self.dp_bits + self.fsdp_bits

    def order(self, c):
        dp = [("dp", k) for k in range(self.dp_bits)]
        fsdp = [("fsdp", k) for k in range(self.fsdp_bits)]
        if c % 2 == 0:
            return dp + fsdp
        return dp[:1] + fsdp + dp[1:]

    def shapes(self, c):
        out, blocks, rows = [], self.n_dp, self.rank
        for axis, _ in self.order(c):
            if axis == "dp":
                blocks //= 2
            else:
                rows //= 2
            out.append((blocks, rows))
        return out


def reduce_kernel(plan, *refs):
    (gq, gk, gv, proj_q, proj_k, proj_v, avg_q, avg_k, avg_v, sq_q, sq_k, sq_v,
     upd_q, upd_k, upd_v, scaled_q, scaled_k, scaled_v) = refs[:18]
    rest = list(refs[18:])
    (turned, acc, grads, held, sums_dp, sums_fsdp, g_sem, s_sem, r_sem, a_send, a_recv,
     d_send, d_recv, f_send, f_recv, out_sem) = rest[:16]
    rest = rest[16:]
    landing, staging = {}, {}
    for c in range(plan.chunks):
        for s in range(plan.stages):
            landing[c, s] = rest.pop(0)
            if s in CODED:
                staging[c, s] = rest.pop(0)

    n_dp, n_fsdp, width, half = plan.n_dp, plan.n_fsdp, plan.width, plan.half
    me_d, me_f = lax.axis_index("dp"), lax.axis_index("fsdp")

    def bit_of(axis, k):
        return ((me_d if axis == "dp" else me_f) // (1 << k)) % 2

    def partner(axis, k):
        step = (1 - 2 * bit_of(axis, k)) * (1 << k)
        return (me_d + step, me_f) if axis == "dp" else (me_d, me_f + step)

    steps = [(c, j) for c in range(plan.chunks) for j in range(n_dp)]
    core = bit_of("dp", 0)

    def fetches(t):
        c, j = steps[t]
        slot = t % PREFETCH
        low = (1 - core) if j < half else core
        block = low + 2 * bit_reverse(j % half, plan.dp_bits - 1)
        if c < plan.n_q:
            start = pl.multiple_of(block * plan.q_cols + c * width, 128)
            return [pltpu.make_async_copy(
                gq.at[0, :, pl.ds(start, width)], grads.at[slot], g_sem.at[slot, 0])]
        start = pl.multiple_of(block * plan.kv_cols, 128)
        return [
            pltpu.make_async_copy(
                g.at[0, :, pl.ds(start, plan.kv_cols)],
                grads.at[slot, :, pl.ds(at * plan.kv_cols, plan.kv_cols)],
                g_sem.at[slot, at])
            for at, g in enumerate((gk, gv))
        ]

    for t in range(PREFETCH - 1):
        for copy in fetches(t):
            copy.start()

    barrier = pltpu.get_barrier_semaphore()
    for k in range(1, n_dp):
        pl.semaphore_signal(
            barrier, inc=1, device_id=((me_d + k) % n_dp, me_f), device_id_type=MESH)
    for k in range(1, n_fsdp):
        pl.semaphore_signal(
            barrier, inc=1, device_id=(me_d, (me_f + k) % n_fsdp), device_id_type=MESH)
    pl.semaphore_wait(barrier, n_dp + n_fsdp - 2)

    for i, proj in enumerate((proj_q, proj_k, proj_v)):
        flat = proj[...].T
        for f in range(n_fsdp):
            at = bit_reverse(f, plan.fsdp_bits) * plan.rows
            turned[i, at:at + plan.rows, :] = flat[f * plan.rows:(f + 1) * plan.rows]

    state = {c: (0, n_dp, 0, plan.rank) for c in range(plan.chunks)}
    copies = {}

    def start(c, s):
        axis, k = plan.order(c)[s]
        base_b, blocks, base_r, rows = state[c]
        bit = bit_of(axis, k)
        send_b, send_r = base_b, base_r
        if s == 0:
            blocks //= 2
            send_b, base_b = 0, half
        elif axis == "dp":
            blocks //= 2
            send_b, base_b = base_b + (1 - bit) * blocks, base_b + bit * blocks
        else:
            rows //= 2
            send_r, base_r = base_r + (1 - bit) * rows, base_r + bit * rows
            send_r = pl.multiple_of(send_r, 16)
            base_r = pl.multiple_of(base_r, 16)
        state[c] = (base_b, blocks, base_r, rows)
        if s in CODED:
            src = staging[c, s]
            tile = min(rows, 32)
            for b in range(blocks):
                def largest(i, top, b=b):
                    x = acc[c, send_b + b, pl.ds(pl.multiple_of(send_r + i * tile, 16), tile), :]
                    return jnp.maximum(
                        top, jnp.max(jnp.abs(x).reshape(tile // 8, 8, width), axis=0))
                top = lax.fori_loop(
                    0, rows // tile, largest, jnp.zeros((8, width), jnp.float32))
                top = jnp.max(top, axis=0, keepdims=True)
                top = (jnp.maximum(top, 1e-30) * 1.01).astype(jnp.bfloat16)
                src[b, pl.ds(rows, 16), :] = jnp.broadcast_to(top, (16, width))
                inverse = SPAN / top.astype(jnp.float32)

                def write(i, _, b=b, inverse=inverse):
                    x = acc[c, send_b + b, pl.ds(pl.multiple_of(send_r + i * tile, 16), tile), :]
                    src[b, pl.ds(pl.multiple_of(i * tile, 16), tile), :] = encode(x, inverse)
                    return 0
                lax.fori_loop(0, rows // tile, write, 0)
        else:
            src = acc.at[c, pl.ds(send_b, blocks), pl.ds(send_r, rows), :]
        copy = pltpu.make_async_remote_copy(
            src_ref=src, dst_ref=landing[c, s], send_sem=s_sem.at[c, s],
            recv_sem=r_sem.at[c, s], device_id=partner(axis, k), device_id_type=MESH)
        copy.start()
        copies[c, s] = copy

    def finish(c, s):
        base_b, blocks, base_r, rows = state[c]
        copies[c, s].wait_recv()
        got = landing[c, s]
        tile = min(rows, 32)
        for b in range(blocks):
            if s in CODED:
                step = got[b, pl.ds(rows, 16), :].astype(jnp.float32)[:1] * (1.0 / SPAN)

            def add(i, _, b=b):
                at = pl.ds(pl.multiple_of(base_r + i * tile, 16), tile)
                x = got[b, pl.ds(pl.multiple_of(i * tile, 16), tile), :]
                if s in CODED:
                    x = decode(x, step)
                acc[c, base_b + b, at, :] = acc[c, base_b + b, at, :] + x
                return 0
            lax.fori_loop(0, rows // tile, add, 0)
        if s + 1 < plan.stages:
            start(c, s + 1)

    def multiply(t):
        c, j = steps[t]
        slot = t % PREFETCH
        if t + PREFETCH - 1 < len(steps):
            for copy in fetches(t + PREFETCH - 1):
                copy.start()
        for copy in fetches(t):
            copy.wait()
        if c < plan.n_q:
            tile = min(width, 256)

            def part(i, _):
                at = pl.ds(pl.multiple_of(i * tile, 128), tile)
                acc[c, j, :, at] = jnp.dot(
                    turned[0], grads[slot, :, at], preferred_element_type=jnp.float32)
                return 0
            lax.fori_loop(0, width // tile, part, 0)
        else:
            for at in range(2):
                cut = pl.ds(at * plan.kv_cols, plan.kv_cols)
                acc[c, j, :, cut] = jnp.dot(
                    turned[1 + at], grads[slot, :, cut], preferred_element_type=jnp.float32)

    for c in range(plan.chunks):
        for j in range(n_dp):
            multiply(c * n_dp + j)
            if j == half - 1:
                start(c, 0)
        if c > 0:
            finish(c - 1, 0)
    finish(plan.chunks - 1, 0)

    rest_order = [(c, s) for c in range(plan.chunks) for s in range(1, plan.stages)]
    for c, s in sorted(rest_order, key=lambda e: (1.5 * (e[0] // 2) + e[1], e[0])):
        finish(c, s)

    local = jnp.zeros((8, 128), jnp.float32)
    for c in range(plan.chunks):
        base_b, _, base_r, rows = state[c]
        x = acc[c, base_b, pl.ds(base_r, rows), :]
        folded = jnp.sum((x * x).reshape(rows // 8, 8, width), axis=0)
        for i in range(width // 128):
            local = local + folded[:, i * 128:(i + 1) * 128]

    def exchange(value, sums, n, send, recv, peer):
        sums[0] = value
        sent = []
        for k in range(1, n):
            copy = pltpu.make_async_remote_copy(
                src_ref=sums.at[0], dst_ref=sums.at[k], send_sem=send.at[k],
                recv_sem=recv.at[k], device_id=peer(k), device_id_type=MESH)
            copy.start()
            sent.append(copy)
        total = value
        for k, copy in enumerate(sent):
            copy.wait_recv()
            total = total + sums[k + 1]
        return total, sent

    total, sent_d = exchange(
        local, sums_dp, n_dp, d_send, d_recv, lambda k: ((me_d + k) % n_dp, me_f))
    total, sent_f = exchange(
        total, sums_fsdp, n_fsdp, f_send, f_recv, lambda k: (me_d, (me_f + k) % n_fsdp))
    square_sum = jnp.sum(jnp.sum(total, axis=0, keepdims=True), axis=1, keepdims=True)
    threshold = math.sqrt(PROJECT_RANK * (QUERY_OUTPUTS + 2 * KEY_VALUE_OUTS))
    clip = jnp.minimum(1.0, threshold / jnp.sqrt(square_sum + 1e-06))

    rows = plan.rows
    correct_one = 1.0 - 0.9**STEP
    correct_two = 1.0 - 0.95**STEP
    place = pl.multiple_of(bit_reverse(me_f, plan.fsdp_bits) * rows, 16)
    gathers = {}

    def gather_start(c, s):
        k = plan.fsdp_bits - 1 - s
        size = rows << s
        base = pl.multiple_of(bit_reverse(me_f, plan.fsdp_bits) // (1 << s) * size, 16)
        view = held.at[c, pl.ds(base, size), :]
        copy = pltpu.make_async_remote_copy(
            src_ref=view, dst_ref=view, send_sem=a_send.at[c, s], recv_sem=a_recv.at[c, s],
            device_id=partner("fsdp", k), device_id_type=MESH)
        copy.start()
        gathers[c, s] = copy

    def adam(c, cols, avg, sq, kept, at):
        base_b, _, base_r, _ = state[c]
        scaled = clip * acc[c, base_b, pl.ds(base_r, rows), cols]
        kept[:, at] = scaled
        new_avg, new_sq = new_moments(scaled, avg[:, at], sq[:, at])
        update = new_avg / correct_one / (jnp.sqrt(new_sq / correct_two) + 1e-08)
        held[c, pl.ds(place, rows), cols] = update.astype(jnp.bfloat16)

    kv = plan.kv_cols
    for c in range(plan.chunks):
        if c < plan.n_q:
            adam(c, slice(0, width), avg_q, sq_q, scaled_q, slice(c * width, (c + 1) * width))
        else:
            adam(c, slice(0, kv), avg_k, sq_k, scaled_k, slice(0, kv))
            adam(c, slice(kv, 2 * kv), avg_v, sq_v, scaled_v, slice(0, kv))
        gather_start(c, 0)

    stores = []

    def store(c):
        for f in range(n_fsdp):
            there = pl.ds(bit_reverse(f, plan.fsdp_bits) * rows, rows)
            here = pl.ds(f * rows, rows)
            if c < plan.n_q:
                parts = [(held.at[c, there, :], upd_q.at[here, pl.ds(c * width, width)])]
            else:
                parts = [(held.at[c, there, pl.ds(0, kv)], upd_k.at[here, :]),
                         (held.at[c, there, pl.ds(kv, kv)], upd_v.at[here, :])]
            for src, dst in parts:
                copy = pltpu.make_async_copy(src, dst, out_sem.at[len(stores)])
                copy.start()
                stores.append(copy)

    gather_order = [(c, s) for c in range(plan.chunks) for s in range(plan.fsdp_bits)]
    for c, s in sorted(gather_order, key=lambda e: (e[0] + e[1], e[0])):
        gathers[c, s].wait_recv()
        if s + 1 < plan.fsdp_bits:
            gather_start(c, s + 1)
        else:
            store(c)

    for copy in list(copies.values()) + list(gathers.values()) + sent_d + sent_f:
        copy.wait_send()
    for copy in stores:
        copy.wait()


def apply_kernel(*refs):
    (proj, upd, weight, comp, scaled, avg, sq, out, navg, nsq) = (
        refs[3 * i:3 * i + 3] for i in range(10))
    for x, a, s, na, ns in zip(scaled, avg, sq, navg, nsq):
        na[...], ns[...] = new_moments(x[...], a[...], s[...])
    for p, u, w, c, o in zip(proj, upd, weight, comp, out):
        delta = -0.04 * jnp.dot(p[...], u[...], preferred_element_type=jnp.float32)
        o[...] = w[...].astype(jnp.float32) + (delta + c[...].astype(jnp.float32))


def apply_updates(projectors, updates, weights, comps, scaled, avgs, sqs):
    rows = weights[0].shape[0]
    steps = rows // min(rows, 128)

    def tiled(array):
        return pl.BlockSpec((array.shape[0] // steps, array.shape[1]), lambda i: (i, 0))

    def whole(array):
        return pl.BlockSpec(array.shape, lambda i: (0, 0))

    args = (*projectors, *updates, *weights, *comps, *scaled, *avgs, *sqs)
    specs = [whole(a) if 3 <= i < 6 else tiled(a) for i, a in enumerate(args)]
    outs = (*weights, *avgs, *sqs)
    return pl.pallas_call(
        apply_kernel,
        grid=(steps,),
        in_specs=specs,
        out_specs=[tiled(a) for a in outs],
        out_shape=[jax.ShapeDtypeStruct(a.shape, jnp.float32) for a in outs],
        compiler_params=pltpu.CompilerParams(vmem_limit_bytes=62 << 20),
        name="apply_updates",
    )(*args)


def shards(n_dp, n_fsdp, *args):
    gradients, projectors, weights, comps, avgs, squares = (args[3 * i:3 * i + 3] for i in range(6))
    depth, rank = projectors[0].shape
    plan = Plan(n_dp, n_fsdp, rank, depth, weights[0].shape[1], weights[1].shape[1])
    bits = plan.fsdp_bits

    scratch = [
        pltpu.VMEM((3, rank, depth), jnp.bfloat16),
        pltpu.VMEM((plan.chunks, n_dp, rank, plan.width), jnp.float32),
        pltpu.VMEM((PREFETCH, depth, plan.width), jnp.bfloat16),
        pltpu.VMEM((plan.chunks, rank, plan.width), jnp.bfloat16),
        pltpu.VMEM((n_dp, 8, 128), jnp.float32),
        pltpu.VMEM((n_fsdp, 8, 128), jnp.float32),
        pltpu.SemaphoreType.DMA((PREFETCH, 2)),
        pltpu.SemaphoreType.DMA((plan.chunks, plan.stages)),
        pltpu.SemaphoreType.DMA((plan.chunks, plan.stages)),
        pltpu.SemaphoreType.DMA((plan.chunks, bits)),
        pltpu.SemaphoreType.DMA((plan.chunks, bits)),
        pltpu.SemaphoreType.DMA((n_dp,)),
        pltpu.SemaphoreType.DMA((n_dp,)),
        pltpu.SemaphoreType.DMA((n_fsdp,)),
        pltpu.SemaphoreType.DMA((n_fsdp,)),
        pltpu.SemaphoreType.DMA(((plan.n_q + 2) * n_fsdp,)),
    ]
    for c in range(plan.chunks):
        for s, (blocks, rows) in enumerate(plan.shapes(c)):
            if s in CODED:
                scratch += [pltpu.VMEM((blocks, rows + 16, plan.width), jnp.bfloat16)] * 2
            else:
                scratch.append(pltpu.VMEM((blocks, rows, plan.width), jnp.float32))

    any_spec = pl.BlockSpec(memory_space=pl.ANY)
    vmem_spec = pl.BlockSpec(memory_space=pltpu.VMEM)
    columns = [w.shape[1] for w in weights]
    moments = [jax.ShapeDtypeStruct(a.shape, jnp.float32) for a in avgs]
    out = pl.pallas_call(
        functools.partial(reduce_kernel, plan),
        in_specs=[any_spec] * 3 + [vmem_spec] * 9,
        out_specs=[any_spec] * 3 + [vmem_spec] * 3,
        out_shape=[jax.ShapeDtypeStruct((rank, c), jnp.bfloat16) for c in columns] + moments,
        scratch_shapes=scratch,
        compiler_params=pltpu.CompilerParams(
            collective_id=0, has_side_effects=True, vmem_limit_bytes=62 << 20),
        name="project_reduce_gather",
    )(*gradients, *projectors, *avgs, *squares)
    return tuple(apply_updates(projectors, out[:3], weights, comps, out[3:6], avgs, squares))


def solution(mesh):
    n_dp, n_fsdp = mesh.shape["dp"], mesh.shape["fsdp"]
    grad, proj, cell = P("dp", "fsdp", None), P("fsdp", None), P("fsdp", "dp")
    in_specs = (grad,) * 3 + (proj,) * 3 + (cell,) * 12
    return jax.shard_map(
        functools.partial(shards, n_dp, n_fsdp),
        mesh=mesh, in_specs=in_specs, out_specs=(cell,) * 9, check_vma=False)
```
